512 devices in a mesh: ctx: 64 (over z, x_hi, core), tp: 8 (over x_lo, y).
Axes of the slice: x: 4 (x_hi: 2, x_lo: 2; x = x_hi * 2 + x_lo), y: 4, z: 16, core: 2. Of those that a mesh axis runs over, the one named last changes fastest.
Arguments:
- queries: bfloat16 [16384, 3072], P('ctx', 'tp'), may hold values from -64 to 64
- keys: bfloat16 [16384, 1024], P('ctx', 'tp'), may hold values from -12 to 12
- values: bfloat16 [16384, 1024], P('ctx', 'tp'), may hold values from -6 to 6
- out_weight: bfloat16 [3072, 5120], P('tp'), may hold values from -0.4375 to 0.4375
Outputs:
- attn_output: bfloat16 [16384, 5120], P('ctx', 'tp')
The draws below stay inside these ranges and needn't reach their ends.
All inputs are finite; a program needn't handle non-finite values.
Results may differ from the reference program's by a relative error of at most 0.02.
Values may be sent and summed in bfloat16 or wider, within the bound.
No kernel may reach another device: no remote copies, remote signals or barrier semaphores. Data moves between devices by JAX's collectives and lax.ppermute only.
A program may use at most 64 MiB of HBM per device.

```python
import jax
import jax.numpy as jnp
from jax import lax

D = 5120
HEAD_DIM = 128
KV_HEADS = 8
HEADS = 24
GROUP = 3
SPAN = 256
WINDOW = 128
INTER_POS = 511
TOKENS = 16384
N_TP = 8


def shared_keys(key):
    normal_part = jnp.clip(jax.random.normal(jax.random.fold_in(key, 101), (TOKENS, KV_HEADS, HEAD_DIM), jnp.float32), -6.0, 6.0)
    return normal_part


def draw_keys(key, part):
    base_field = shared_keys(key)
    return base_field.reshape(TOKENS, KV_HEADS * HEAD_DIM).astype(jnp.bfloat16)


def draw_queries(key, part):
    key = jax.random.fold_in(key, 5)
    own_field = 2.5 * jnp.clip(jax.random.normal(key, (TOKENS, KV_HEADS, GROUP, HEAD_DIM), jnp.float32), -6.0, 6.0)
    return own_field.reshape(TOKENS, HEADS * HEAD_DIM).astype(jnp.bfloat16)


def steps_of(rng, dims, cuts, smallest, largest):
    gain = 1.0
    for position, shards_of in cuts:
        steps = jax.random.uniform(jax.random.fold_in(jax.random.fold_in(rng, 6), position), (shards_of,), jnp.float32, smallest / len(cuts), largest / len(cuts))
        gain = gain * jnp.repeat(jnp.exp(steps), dims[position] // shards_of).reshape((-1,) + (1,) * (len(dims) - 1 - position))
    return gain


def normal_values(stream_key, extent, scale, bound, shards=(), kind=jnp.bfloat16):
    drawn = jax.random.normal(stream_key, extent, jnp.float32) * scale
    if len(shards) > 0:
        drawn = steps_of(stream_key, extent, shards, -0.22, 0.18) * drawn
    return jnp.clip(drawn, min=-bound, max=bound).astype(kind)


def setup_inputs(seed: int = 0) -> dict:
    streams_of = jax.random.split(jax.random.key(seed), 5)
    queries = draw_queries(jax.random.fold_in(streams_of[4], 71), 0)
    keys = draw_keys(jax.random.fold_in(streams_of[4], 71), 0)
    values = normal_values(streams_of[2], (TOKENS, KV_HEADS * HEAD_DIM), 1.0, 6.0, ((0, 64), (1, 8)))
    out_weight = normal_values(streams_of[3], (HEADS * HEAD_DIM, D), (HEADS * HEAD_DIM // 16) ** -0.5, 0.4375, ((0, 8),))
    return {"queries": queries, "keys": keys, "values": values, "out_weight": out_weight}


rope_base = 10000000.0


def rope_tables(positions, head_dim):
    half_dim = head_dim // 2
    inverse_freq = rope_base ** (-(jnp.arange(half_dim, dtype=jnp.float32) * 2.0) / head_dim)
    angles = positions.astype(jnp.float32)[:, None] * inverse_freq[None, :]
    angles = jnp.concatenate([angles, angles], axis=1)
    return jnp.cos(angles), jnp.sin(angles)


def rotate(vectors, cosine_table, sine_table):
    half_dim = vectors.shape[-1] // 2
    turned = jnp.concatenate([-vectors[..., half_dim:], vectors[..., :half_dim]], axis=-1)
    spread_shape = (cosine_table.shape[0],) + (1,) * (vectors.ndim - 2) + (cosine_table.shape[1],)
    return vectors * cosine_table.reshape(spread_shape) + turned * sine_table.reshape(spread_shape)


def query_positions(offset_in_span):
    intra = offset_in_span
    successive = jnp.where(offset_in_span < WINDOW, SPAN + offset_in_span, INTER_POS)
    inter = jnp.zeros_like(offset_in_span) + INTER_POS
    return intra, successive, inter


def stored(vectors):
    return lax.optimization_barrier(vectors.astype(jnp.bfloat16)).astype(jnp.float32)


def reference(queries, keys, values, out_weight):
    span_total = TOKENS // SPAN
    row_index = jnp.arange(TOKENS, dtype=jnp.int32)
    key_cosine, key_sine = rope_tables(row_index % SPAN, HEAD_DIM)
    keys_rot = stored(rotate(keys.astype(jnp.float32).reshape(TOKENS, KV_HEADS, HEAD_DIM), key_cosine, key_sine))
    values_all = values.astype(jnp.float32).reshape(TOKENS, KV_HEADS, HEAD_DIM)
    key_span = row_index // SPAN
    offsets = jnp.arange(SPAN, dtype=jnp.int32)
    tables = [rope_tables(position_table, HEAD_DIM) for position_table in query_positions(offsets)]
    causal = offsets[:, None] >= offsets[None, :]
    scale = 1.0 / (HEAD_DIM ** 0.5)
    highest_precision = lax.Precision.HIGHEST

    def one_span(span_index):
        row_start = span_index * SPAN
        block_queries = lax.dynamic_slice_in_dim(queries, row_start, SPAN, 0).astype(jnp.float32)
        block_queries = block_queries.reshape(SPAN, KV_HEADS, GROUP, HEAD_DIM)
        rotated = [stored(rotate(block_queries, cosine_table, sine_table)) for cosine_table, sine_table in tables]
        own_keys = lax.dynamic_slice_in_dim(keys_rot, row_start, SPAN, 0)
        own_values = lax.dynamic_slice_in_dim(values_all, row_start, SPAN, 0)
        prior_start = jnp.maximum(span_index - 1, 0) * SPAN
        prior_keys = lax.dynamic_slice_in_dim(keys_rot, prior_start, SPAN, 0)
        prior_values = lax.dynamic_slice_in_dim(values_all, prior_start, SPAN, 0)
        scores = jnp.concatenate([
            jnp.einsum('tkgd,jkd->kgtj', rotated[0], own_keys, precision=highest_precision),
            jnp.einsum('tkgd,jkd->kgtj', rotated[1], prior_keys, precision=highest_precision),
            jnp.einsum('tkgd,jkd->kgtj', rotated[2], keys_rot, precision=highest_precision)], axis=-1) * scale
        allowed = jnp.concatenate([
            causal,
            jnp.broadcast_to(span_index >= 1, (SPAN, SPAN)),
            jnp.broadcast_to((key_span <= span_index - 2)[None, :], (SPAN, TOKENS))], axis=1)
        scores = jnp.where(allowed, scores, -jnp.inf)
        highest = jnp.max(scores, axis=-1, keepdims=True)
        raw = jnp.where(allowed, jnp.exp(scores - highest), 0.0)
        weight_sum = jnp.sum(raw, axis=-1)
        joined_values = jnp.concatenate([own_values, prior_values, values_all], axis=0)
        mixed = jnp.einsum('kgtj,jkd->kgtd', stored(raw), joined_values, precision=highest_precision)
        mixed = mixed / weight_sum[..., None]
        return mixed.transpose(2, 0, 1, 3).reshape(SPAN, HEADS * HEAD_DIM).astype(jnp.bfloat16)

    attended = lax.map(one_span, jnp.arange(span_total, dtype=jnp.int32)).reshape(TOKENS, HEADS * HEAD_DIM)
    group_width = HEADS * HEAD_DIM // N_TP

    def add_group(summed, group_index):
        head_columns = lax.dynamic_slice_in_dim(attended, group_index * group_width, group_width, 1).astype(jnp.float32)
        weight_rows = lax.dynamic_slice_in_dim(out_weight, group_index * group_width, group_width, 0).astype(jnp.float32)
        partial_sum = jnp.dot(head_columns, weight_rows, preferred_element_type=jnp.float32, precision=highest_precision)
        return summed + stored(partial_sum), None

    summed, _ = lax.scan(add_group, jnp.zeros((TOKENS, D), jnp.float32), jnp.arange(N_TP, dtype=jnp.int32))
    return summed.astype(jnp.bfloat16)
```

```python
import functools

import jax
import jax.numpy as jnp
import numpy as np
from jax import lax
from jax.experimental import pallas as pl
from jax.experimental.pallas import tpu as pltpu
from jax.sharding import PartitionSpec as P

HEAD_DIM = 128
SPAN = 256
WINDOW = 128
INTER_POS = 511
GROUP = 3
ROWS = GROUP * SPAN
ROPE_BASE = 10000000.0
FLOOR = -1e30
SCALE = float(np.log2(np.e) / np.sqrt(HEAD_DIM))
BF = jnp.bfloat16
F32 = jnp.float32
VMEM = pl.BlockSpec(memory_space=pltpu.VMEM)
SMEM = pl.BlockSpec(memory_space=pltpu.SMEM)
PART_ROWS = ROWS + 16 * GROUP

N_Z, N_ZH, N_ZL = 16, 4, 4
STEPS = (-1, 1, 2)
CTX = 64
TP = 8


def rope_tables():
    half = HEAD_DIM // 2
    freq = np.float32(ROPE_BASE) ** (-(np.arange(half, dtype=np.float32) * np.float32(2.0)) / np.float32(HEAD_DIM))
    freq = freq.astype(np.float32)

    def table(positions):
        angles = (positions.astype(np.float32)[:, None] * freq[None, :]).astype(np.float32)
        return np.concatenate([np.cos(angles), np.sin(angles)], axis=1).astype(np.float32)

    offset = np.arange(SPAN)
    succ = np.where(offset < WINDOW, SPAN + offset, INTER_POS)
    inter = np.full((8,), INTER_POS)
    return table(offset), table(succ), table(inter)


def full_tables(table):
    lane = lax.broadcasted_iota(jnp.int32, table.shape, 1)
    turned = pltpu.roll(table, HEAD_DIM // 2, 1)
    first = lane < HEAD_DIM // 2
    return jnp.where(first, table, turned), jnp.where(first, -turned, table)


def rotated(x, tables):
    return x * tables[0] + pltpu.roll(x, HEAD_DIM // 2, 1) * tables[1]


def prepare_kernel(queries, keys, values, own, succ, inter, kv, q_pair, q_intra):
    own_tables = full_tables(own[...])
    kv[:SPAN, :] = rotated(keys[...].astype(F32), own_tables).astype(BF)
    kv[SPAN:, :] = values[...]
    succ_tables = full_tables(succ[...])
    inter_tables = [jnp.broadcast_to(t[0:1, :], (SPAN, HEAD_DIM)) for t in full_tables(inter[...])]
    for h in range(GROUP):
        x = queries[:, h * HEAD_DIM:(h + 1) * HEAD_DIM].astype(F32)
        rows = slice(h * SPAN, (h + 1) * SPAN)
        q_pair[0, rows, :] = rotated(x, inter_tables).astype(BF)
        q_pair[1, rows, :] = rotated(x, succ_tables).astype(BF)
        q_intra[rows, :] = rotated(x, own_tables).astype(BF)


def prepare(*operands):
    def whole(x):
        return pl.BlockSpec(x.shape, lambda i: (0,) * len(x.shape))

    outs = (shape((2 * SPAN, HEAD_DIM), BF), shape((2, ROWS, HEAD_DIM), BF), shape((ROWS, HEAD_DIM), BF))
    return pl.pallas_call(
        prepare_kernel,
        grid=(1,),
        out_shape=outs,
        in_specs=[whole(x) for x in operands],
        out_specs=tuple(whole(x) for x in outs),
        compiler_params=pltpu.CompilerParams(vmem_limit_bytes=60 * 1024 * 1024),
        cost_estimate=pl.CostEstimate(flops=10 ** 6, bytes_accessed=2 ** 20, transcendentals=0),
    )(*operands)


def scores(q, k):
    return lax.dot_general(q, k, (((1,), (1,)), ((), ())), preferred_element_type=F32)


def absorb(state, q, k, v, mask=None):
    top, total, summed = state
    lanes = k.shape[0] // HEAD_DIM
    s = scores(q[...], k)
    if mask is not None:
        s = jnp.where(mask, s, FLOOR)
    peak = s[:, :HEAD_DIM]
    for i in range(1, lanes):
        peak = jnp.maximum(peak, s[:, i * HEAD_DIM:(i + 1) * HEAD_DIM])
    old = top[...]
    new = jnp.maximum(old, jnp.max(peak, axis=1, keepdims=True))
    base = new * SCALE
    fade = jnp.exp2(old * SCALE - base)
    parts = []
    mass = total[...] * fade
    for i in range(lanes):
        w = jnp.exp2(s[:, i * HEAD_DIM:(i + 1) * HEAD_DIM] * SCALE - base)
        if mask is not None:
            w = jnp.where(mask[:, i * HEAD_DIM:(i + 1) * HEAD_DIM], w, 0.0)
        mass = mass + w
        parts.append(w.astype(BF))
    w = jnp.concatenate(parts, axis=1)
    top[...] = new
    total[...] = mass
    summed[...] = summed[...] * fade + jnp.dot(w, v, preferred_element_type=F32)


def absorb_buffer(state, span, q_ref, buf, row, first, step):
    low = jnp.minimum(first, first + 3 * step)
    count = jnp.clip((span - 2 - low + 64) // 16 - 3, 0, 4)
    start = jnp.where(step > 0, 0, 4 - count)

    def block(j):
        return pl.multiple_of(row + j * (2 * SPAN), 2 * SPAN)

    for size in (4, 3):
        @pl.when(count == size)
        def _(size=size):
            k = jnp.concatenate([buf[pl.ds(block(start + j), SPAN), :] for j in range(size)], axis=0)
            v = jnp.concatenate(
                [buf[pl.ds(pl.multiple_of(block(start + j) + SPAN, SPAN), SPAN), :] for j in range(size)], axis=0)
            absorb(state, q_ref.at[0], k, v)

    def one(j, carry):
        distance = span - (first + step * j)

        @pl.when(jnp.logical_or(distance == 1, jnp.logical_and(distance >= 2, count < 3)))
        def _():
            kind = jnp.where(distance == 1, 1, 0)
            k = buf[pl.ds(block(j), SPAN), :]
            v = buf[pl.ds(pl.multiple_of(block(j) + SPAN, SPAN), SPAN), :]
            absorb(state, q_ref.at[kind], k, v)

        return carry

    lax.fori_loop(0, N_ZH, one, 0)


def spans_of(place, step, other):
    core = lax.rem(place, 2)
    which = 1 - core if other else core
    residue = lax.rem(place // 4 + step + N_Z, N_ZL)
    first = residue * 4 + lax.rem(place // 2, 2) * 2 + which
    return first + jnp.where(which == 1, 48, 0), jnp.where(which == 1, -16, 16)


def targets_of(place):
    return place, place + 2 - 4 * lax.rem(place // 2, 2)


def pick(values, i):
    result = values[-1]
    for j in range(len(values) - 2, -1, -1):
        result = jnp.where(i == j, values[j], result)
    return result


def absorb_all(targets, segments, q_of, buf, states):
    size = N_ZH * 2 * SPAN
    count = len(segments)

    def one(i, carry):
        target, segment = i // count, lax.rem(i, count)
        absorb_buffer(
            [x.at[target] for x in states], pick(targets, target), q_of(target), buf, segment * size,
            pick([first for first, _ in segments], segment), pick([step for _, step in segments], segment),
        )
        return carry

    lax.fori_loop(0, len(targets) * count, one, 0)


def copy_all(sources, target):
    at = 0
    for source in sources:
        target[at:at + source.shape[0]] = source[...]
        at += source.shape[0]


def first_kernel(place, q_own, q_peer, q_intra, kv, far, far_other, top, total, summed, done, q_all, joined):
    done[...] = jnp.zeros(done.shape, F32)
    states = (top, total, summed)
    top[...] = jnp.full(top.shape, FLOOR, F32)
    total[...] = jnp.zeros(total.shape, F32)
    summed[...] = jnp.zeros(summed.shape, F32)
    q_all[0] = q_own[...]
    q_all[1] = q_peer[...]
    copy_all([far, far_other], joined)
    row = lax.broadcasted_iota(jnp.int32, (ROWS, SPAN), 0) % SPAN
    column = lax.broadcasted_iota(jnp.int32, (ROWS, SPAN), 1)
    absorb([x.at[0] for x in states], q_intra, kv[:SPAN, :], kv[SPAN:, :], mask=row >= column)
    here = place[0]
    absorb_all(targets_of(here), [spans_of(here, 0, False), spans_of(here, 0, True)], lambda i: q_all.at[i], joined, states)


def near_kernel(steps, place, q_own, q_peer, before, *refs):
    bufs, ins, states = refs[:len(steps)], refs[len(steps):len(steps) + 3], refs[len(steps) + 3:len(steps) + 6]
    done, joined, q_all = refs[len(steps) + 6:]
    done[...] = before[...]
    for source, target in zip(ins, states):
        target[...] = source[...]
    q_all[0] = q_own[...]
    q_all[1] = q_peer[...]
    copy_all(bufs, joined)
    here = place[0]
    absorb_all(targets_of(here), [spans_of(here, step, False) for step in steps], lambda i: q_all.at[i], joined, states)


def three_terms(x):
    hi = x.astype(BF)
    rest = x - hi.astype(F32)
    mid = rest.astype(BF)
    low = (rest - mid.astype(F32)).astype(BF)
    return hi, mid, low


def last_segments(place):
    return [spans_of(place, step, True) for step in STEPS]


def peer_kernel(place, q_peer, two, three, *refs):
    ins, out, state, joined = refs[:3], refs[3], refs[4:7], refs[7]
    for source, target in zip(ins, state):
        target[0] = source[1]
    copy_all([two, three], joined)
    here = place[0]
    absorb_all(targets_of(here)[1:], last_segments(here), lambda i: q_peer, joined, state)
    state = [x.at[0] for x in state]
    lane = lax.broadcasted_iota(jnp.int32, (SPAN, HEAD_DIM), 1)
    for h in range(GROUP):
        rows = slice(h * SPAN, (h + 1) * SPAN)
        mass = jnp.sum(state[1][rows, :], axis=1, keepdims=True)
        safe = jnp.where(mass > 0.0, mass, 1.0)
        out[rows, :] = (state[2][rows, :] / safe).astype(BF)
        stats = jnp.zeros((SPAN, HEAD_DIM), F32)
        terms = three_terms(state[0][rows, :]) + three_terms(jnp.broadcast_to(mass, (SPAN, HEAD_DIM)))
        for i, term in enumerate(terms):
            stats = jnp.where(lane == i, term.astype(F32), stats)
        stats = stats.T
        both = jnp.concatenate([stats[:8, :HEAD_DIM], stats[:8, HEAD_DIM:]], axis=0)
        out[ROWS + 16 * h:ROWS + 16 * (h + 1), :] = both.astype(BF)


def own_kernel(place, q_own, two, three, *refs):
    ins, outs, joined = refs[:3], refs[3:6], refs[6]
    for source, target in zip(ins, outs):
        target[...] = source[0:1]
    copy_all([two, three], joined)
    here = place[0]
    absorb_all(targets_of(here)[:1], last_segments(here), lambda i: q_own, joined, outs)


def merge(top, total, summed, part, out):
    for h in range(GROUP):
        rows = slice(h * SPAN, (h + 1) * SPAN)
        both = part[ROWS + 16 * h:ROWS + 16 * (h + 1), :].astype(F32)
        stats = jnp.concatenate([both[:8, :], both[8:, :]], axis=1)
        stats = jnp.concatenate([stats, jnp.zeros((HEAD_DIM - 8, SPAN), F32)], axis=0).T
        other_top = stats[:, 0:1] + stats[:, 1:2] + stats[:, 2:3]
        other_mass = stats[:, 3:4] + stats[:, 4:5] + stats[:, 5:6]
        own_top = top[rows, :][:, 0:1]
        own_mass = jnp.sum(total[rows, :], axis=1, keepdims=True)
        peak = jnp.maximum(own_top, other_top)
        own_scale = jnp.exp2((own_top - peak) * SCALE)
        other_scale = jnp.exp2((other_top - peak) * SCALE) * other_mass
        norm = 1.0 / (own_mass * own_scale + other_scale)
        value = summed[rows, :] * (own_scale * norm) + part[rows, :].astype(F32) * (other_scale * norm)
        out[:, h * HEAD_DIM:(h + 1) * HEAD_DIM] = value.astype(BF)


def project_kernel(top, total, summed, part, weight, out, attended):
    @pl.when(pl.program_id(0) == 0)
    def _():
        merge(top.at[0], total.at[0], summed.at[0], part, attended)

    out[0] = jnp.dot(attended[...], weight[...], preferred_element_type=F32).astype(BF)


def project(state, part, weight):
    depth, width = weight.shape[0], weight.shape[1] // TP
    whole = pl.BlockSpec((1, ROWS, HEAD_DIM), lambda t: (0, 0, 0))
    return pl.pallas_call(
        project_kernel,
        grid=(TP,),
        out_shape=shape((TP, SPAN, width), BF),
        in_specs=[whole] * 3 + [
            pl.BlockSpec((PART_ROWS, HEAD_DIM), lambda t: (0, 0)), pl.BlockSpec((depth, width), lambda t: (0, t))
        ],
        out_specs=pl.BlockSpec((1, SPAN, width), lambda t: (t, 0, 0)),
        scratch_shapes=[pltpu.VMEM((SPAN, depth), BF)],
        compiler_params=pltpu.CompilerParams(vmem_limit_bytes=16 * 1024 * 1024),
        cost_estimate=pl.CostEstimate(
            flops=2 * SPAN * depth * TP * width, bytes_accessed=2 * TP * width * (depth + SPAN), transcendentals=0),
    )(*state, part, weight)


def sum_kernel(parts, out):
    total = parts[0].astype(F32)
    for t in range(1, TP):
        total = total + parts[t].astype(F32)
    out[...] = total.astype(BF)


def sum_parts(parts):
    _, rows, width = parts.shape
    block = rows // 4
    return pl.pallas_call(
        sum_kernel,
        grid=(4,),
        out_shape=shape((rows, width), BF),
        in_specs=[pl.BlockSpec((TP, block, width), lambda t: (0, t, 0))],
        out_specs=pl.BlockSpec((block, width), lambda t: (t, 0)),
        compiler_params=pltpu.CompilerParams(vmem_limit_bytes=12 * 1024 * 1024),
        cost_estimate=pl.CostEstimate(flops=TP * rows * width, bytes_accessed=2 * TP * rows * width, transcendentals=0),
    )(parts)


def call(kernel, outs, operands, flops, scratch=(), smem_first=True):
    specs = [VMEM] * len(operands)
    if smem_first:
        specs[0] = SMEM
    nbytes = sum(int(np.prod(x.shape)) * x.dtype.itemsize for x in list(operands) + list(outs))
    result = pl.pallas_call(
        kernel,
        out_shape=tuple(outs),
        in_specs=specs,
        out_specs=tuple([VMEM] * len(outs)),
        scratch_shapes=list(scratch),
        compiler_params=pltpu.CompilerParams(vmem_limit_bytes=18 * 1024 * 1024),
        cost_estimate=pl.CostEstimate(flops=flops, bytes_accessed=nbytes, transcendentals=0),
    )(*operands)
    return result


def shape(dims, dtype):
    return jax.ShapeDtypeStruct(dims, dtype)


def z_route(core0, core1):
    route = []
    for z in range(N_Z):
        for r in range(4):
            d = core1 if r % 2 else core0
            route.append((z * 4 + r, ((z + d) % N_Z) * 4 + r))
    return route


SWAP_CORE = [(i, i ^ 1) for i in range(CTX)]
SWAP_HI = [(i, i ^ 2) for i in range(CTX)]
FAR_GROUPS = [
    [a * 16 + r for a in (range(N_ZH) if r % 2 == 0 else reversed(range(N_ZH)))] for r in range(16)
]


def local(queries, keys, values, out_weight):
    own_table, succ_table, inter_table = (jnp.asarray(t) for t in rope_tables())
    place = lax.axis_index("ctx").astype(jnp.int32).reshape(1)

    kv, q_own, q_intra = prepare(queries, keys, values, own_table, succ_table, inter_table)
    q_peer = lax.ppermute(q_own, "ctx", SWAP_HI)
    far = lax.all_gather(kv, "ctx", axis=0, tiled=True, axis_index_groups=FAR_GROUPS)
    far, q_peer = lax.optimization_barrier((far, q_peer))
    near = [
        lax.ppermute(far, "ctx", z_route(1, 1)),
        lax.ppermute(far, "ctx", z_route(-1, -1)),
        lax.ppermute(far, "ctx", z_route(2, -2)),
    ]
    far_other = lax.ppermute(far, "ctx", SWAP_CORE)

    state_shapes = [shape((1, ROWS, HEAD_DIM), F32)] * 3
    both_shapes = [shape((2, ROWS, HEAD_DIM), F32)] * 3
    token = shape((8, HEAD_DIM), F32)
    tile = 4 * ROWS * SPAN * HEAD_DIM
    size = far.shape[0]
    q_scratch = pltpu.VMEM((2, 2, ROWS, HEAD_DIM), BF)

    *state, done = call(
        first_kernel, both_shapes + [token], [place, q_own, q_peer, q_intra, kv, far, far_other], 17 * tile,
        scratch=[q_scratch, pltpu.VMEM((2 * size, HEAD_DIM), BF)],
    )
    *near[:2], done = lax.optimization_barrier((*near[:2], done))
    *state, done, joined = call(
        functools.partial(near_kernel, STEPS[:2]), both_shapes + [token, shape((2 * size, HEAD_DIM), BF)],
        [place, q_own, q_peer, done] + near[:2] + state, 16 * tile, scratch=[q_scratch],
    )
    two = lax.ppermute(joined, "ctx", SWAP_CORE)
    near[2], done = lax.optimization_barrier((near[2], done))
    three = lax.ppermute(near[2], "ctx", SWAP_CORE)
    *state, _, _ = call(
        functools.partial(near_kernel, STEPS[2:]), both_shapes + [token, shape((size, HEAD_DIM), BF)],
        [place, q_own, q_peer, done] + near[2:] + state, 8 * tile, scratch=[q_scratch],
    )
    last_scratch = pltpu.VMEM((3 * size, HEAD_DIM), BF)
    (part,) = call(
        peer_kernel, [shape((PART_ROWS, HEAD_DIM), BF)], [place, q_peer, two, three] + state, 12 * tile,
        scratch=[pltpu.VMEM((1, ROWS, HEAD_DIM), F32)] * 3 + [last_scratch],
    )
    part_here = lax.ppermute(part, "ctx", SWAP_HI)
    own = call(own_kernel, state_shapes, [place, q_own, two, three] + state, 12 * tile, scratch=[last_scratch])
    partial = project(own, part_here, out_weight)
    return sum_parts(lax.all_to_all(partial, "tp", 0, 0))


def solution(mesh):
    placed = (P("ctx", "tp"), P("ctx", "tp"), P("ctx", "tp"), P("tp", None))
    return jax.shard_map(
        local, mesh=mesh, in_specs=placed, out_specs=P("ctx", "tp"), check_vma=False
    )
```

```python
import functools

import jax
import jax.numpy as jnp
import numpy as np
from jax import lax
from jax.experimental import pallas as pl
from jax.experimental.pallas import tpu as pltpu
from jax.sharding import PartitionSpec as P

HEAD_DIM = 128
SPAN = 256
WINDOW = 128
INTER_POS = 511
GROUP = 3
ROWS = GROUP * SPAN
ROPE_BASE = 10000000.0
FLOOR = -1e30
SCALE = float(np.log2(np.e) / np.sqrt(HEAD_DIM))
BF = jnp.bfloat16
F32 = jnp.float32
VMEM = pl.BlockSpec(memory_space=pltpu.VMEM)
SMEM = pl.BlockSpec(memory_space=pltpu.SMEM)
PART_ROWS = ROWS + 16 * GROUP

N_Z, N_ZH, N_ZL = 16, 4, 4
STEPS = (-1, 1, 2)
CTX = 64
TP = 8


def rope_tables():
    half = HEAD_DIM // 2
    freq = np.float32(ROPE_BASE) ** (-(np.arange(half, dtype=np.float32) * np.float32(2.0)) / np.float32(HEAD_DIM))
    freq = freq.astype(np.float32)

    def table(positions):
        angles = (positions.astype(np.float32)[:, None] * freq[None, :]).astype(np.float32)
        return np.concatenate([np.cos(angles), np.sin(angles)], axis=1).astype(np.float32)

    offset = np.arange(SPAN)
    succ = np.where(offset < WINDOW, SPAN + offset, INTER_POS)
    inter = np.full((8,), INTER_POS)
    return table(offset), table(succ), table(inter)


def full_tables(table):
    lane = lax.broadcasted_iota(jnp.int32, table.shape, 1)
    turned = pltpu.roll(table, HEAD_DIM // 2, 1)
    first = lane < HEAD_DIM // 2
    return jnp.where(first, table, turned), jnp.where(first, -turned, table)


def rotated(x, tables):
    return x * tables[0] + pltpu.roll(x, HEAD_DIM // 2, 1) * tables[1]


def prepare_kernel(queries, keys, values, own, succ, inter, weight, kv, q_pair, q_intra, blocks, sems):
    width = blocks.shape[2]
    copies = [
        pltpu.make_async_copy(weight.at[:, t * width:(t + 1) * width], blocks.at[t], sems.at[t]) for t in range(TP)
    ]
    for copy in copies:
        copy.start()
    own_tables = full_tables(own[...])
    kv[:SPAN, :] = rotated(keys[...].astype(F32), own_tables).astype(BF)
    kv[SPAN:, :] = values[...]
    succ_tables = full_tables(succ[...])
    inter_tables = [jnp.broadcast_to(t[0:1, :], (SPAN, HEAD_DIM)) for t in full_tables(inter[...])]
    for h in range(GROUP):
        x = queries[:, h * HEAD_DIM:(h + 1) * HEAD_DIM].astype(F32)
        rows = slice(h * SPAN, (h + 1) * SPAN)
        q_pair[0, rows, :] = rotated(x, inter_tables).astype(BF)
        q_pair[1, rows, :] = rotated(x, succ_tables).astype(BF)
        q_intra[rows, :] = rotated(x, own_tables).astype(BF)
    for copy in copies:
        copy.wait()


def prepare(*operands):
    def whole(x):
        return pl.BlockSpec(x.shape, lambda i: (0,) * len(x.shape))

    depth, width = operands[-1].shape[0], operands[-1].shape[1] // TP
    outs = (
        shape((2 * SPAN, HEAD_DIM), BF), shape((2, ROWS, HEAD_DIM), BF), shape((ROWS, HEAD_DIM), BF),
        shape((TP, depth, width), BF),
    )
    return pl.pallas_call(
        prepare_kernel,
        grid=(1,),
        out_shape=outs,
        in_specs=[whole(x) for x in operands[:-1]] + [pl.BlockSpec(memory_space=pl.ANY)],
        out_specs=tuple(whole(x) for x in outs),
        scratch_shapes=[pltpu.SemaphoreType.DMA((TP,))],
        compiler_params=pltpu.CompilerParams(vmem_limit_bytes=60 * 1024 * 1024),
        cost_estimate=pl.CostEstimate(flops=10 ** 6, bytes_accessed=2 ** 23, transcendentals=0),
    )(*operands)


def scores(q, k):
    return lax.dot_general(q, k, (((1,), (1,)), ((), ())), preferred_element_type=F32)


def absorb(state, q, k, v, mask=None):
    top, total, summed = state
    lanes = k.shape[0] // HEAD_DIM
    s = scores(q[...], k)
    if mask is not None:
        s = jnp.where(mask, s, FLOOR)
    peak = s[:, :HEAD_DIM]
    for i in range(1, lanes):
        peak = jnp.maximum(peak, s[:, i * HEAD_DIM:(i + 1) * HEAD_DIM])
    old = top[...]
    new = jnp.maximum(old, jnp.max(peak, axis=1, keepdims=True))
    base = new * SCALE
    fade = jnp.exp2(old * SCALE - base)
    parts = []
    mass = total[...] * fade
    for i in range(lanes):
        w = jnp.exp2(s[:, i * HEAD_DIM:(i + 1) * HEAD_DIM] * SCALE - base)
        if mask is not None:
            w = jnp.where(mask[:, i * HEAD_DIM:(i + 1) * HEAD_DIM], w, 0.0)
        mass = mass + w
        parts.append(w.astype(BF))
    w = jnp.concatenate(parts, axis=1)
    top[...] = new
    total[...] = mass
    summed[...] = summed[...] * fade + jnp.dot(w, v, preferred_element_type=F32)


def absorb_buffer(state, span, q_ref, buf, row, first, step):
    low = jnp.minimum(first, first + 3 * step)
    count = jnp.clip((span - 2 - low + 64) // 16 - 3, 0, 4)
    start = jnp.where(step > 0, 0, 4 - count)

    def block(j):
        return pl.multiple_of(row + j * (2 * SPAN), 2 * SPAN)

    for size in (4, 3):
        @pl.when(count == size)
        def _(size=size):
            k = jnp.concatenate([buf[pl.ds(block(start + j), SPAN), :] for j in range(size)], axis=0)
            v = jnp.concatenate(
                [buf[pl.ds(pl.multiple_of(block(start + j) + SPAN, SPAN), SPAN), :] for j in range(size)], axis=0)
            absorb(state, q_ref.at[0], k, v)

    def one(j, carry):
        distance = span - (first + step * j)

        @pl.when(jnp.logical_or(distance == 1, jnp.logical_and(distance >= 2, count < 3)))
        def _():
            kind = jnp.where(distance == 1, 1, 0)
            k = buf[pl.ds(block(j), SPAN), :]
            v = buf[pl.ds(pl.multiple_of(block(j) + SPAN, SPAN), SPAN), :]
            absorb(state, q_ref.at[kind], k, v)

        return carry

    lax.fori_loop(0, N_ZH, one, 0)


def spans_of(place, step, other):
    core = lax.rem(place, 2)
    which = 1 - core if other else core
    residue = lax.rem(place // 4 + step + N_Z, N_ZL)
    first = residue * 4 + lax.rem(place // 2, 2) * 2 + which
    return first + jnp.where(which == 1, 48, 0), jnp.where(which == 1, -16, 16)


def targets_of(place):
    return place, place + 2 - 4 * lax.rem(place // 2, 2)


def pick(values, i):
    result = values[-1]
    for j in range(len(values) - 2, -1, -1):
        result = jnp.where(i == j, values[j], result)
    return result


def absorb_all(targets, segments, q_of, buf, states):
    size = N_ZH * 2 * SPAN
    count = len(segments)

    def one(i, carry):
        target, segment = i // count, lax.rem(i, count)
        absorb_buffer(
            [x.at[target] for x in states], pick(targets, target), q_of(target), buf, segment * size,
            pick([first for first, _ in segments], segment), pick([step for _, step in segments], segment),
        )
        return carry

    lax.fori_loop(0, len(targets) * count, one, 0)


def copy_all(sources, target):
    at = 0
    for source in sources:
        target[at:at + source.shape[0]] = source[...]
        at += source.shape[0]


def first_kernel(place, q_own, q_peer, q_intra, kv, far, far_other, top, total, summed, done, q_all, joined):
    done[...] = jnp.zeros(done.shape, F32)
    states = (top, total, summed)
    top[...] = jnp.full(top.shape, FLOOR, F32)
    total[...] = jnp.zeros(total.shape, F32)
    summed[...] = jnp.zeros(summed.shape, F32)
    q_all[0] = q_own[...]
    q_all[1] = q_peer[...]
    copy_all([far, far_other], joined)
    row = lax.broadcasted_iota(jnp.int32, (ROWS, SPAN), 0) % SPAN
    column = lax.broadcasted_iota(jnp.int32, (ROWS, SPAN), 1)
    absorb([x.at[0] for x in states], q_intra, kv[:SPAN, :], kv[SPAN:, :], mask=row >= column)
    here = place[0]
    absorb_all(targets_of(here), [spans_of(here, 0, False), spans_of(here, 0, True)], lambda i: q_all.at[i], joined, states)


def near_kernel(place, q_own, q_peer, before, low, high, *refs):
    ins, states, (done, joined, q_all) = refs[:3], refs[3:6], refs[6:]
    done[...] = before[...]
    for source, target in zip(ins, states):
        target[...] = source[...]
    q_all[0] = q_own[...]
    q_all[1] = q_peer[...]
    copy_all([low, high], joined)
    here = place[0]
    absorb_all(
        targets_of(here), [spans_of(here, step, False) for step in STEPS[:2]], lambda i: q_all.at[i], joined, states)


def near_peer_kernel(place, q_peer, near, *refs):
    ins, states = refs[:3], refs[3:6]
    for source, target in zip(ins, states):
        target[...] = source[1:2]
    here = place[0]
    absorb_all(targets_of(here)[1:], [spans_of(here, STEPS[2], False)], lambda i: q_peer, near, states)


def three_terms(x):
    hi = x.astype(BF)
    rest = x - hi.astype(F32)
    mid = rest.astype(BF)
    low = (rest - mid.astype(F32)).astype(BF)
    return hi, mid, low


def last_segments(place):
    return [spans_of(place, step, True) for step in STEPS] + [spans_of(place, STEPS[2], False)]


def peer_kernel(place, q_peer, two, three, *refs):
    ins, out, state, joined = refs[:3], refs[3], refs[4:7], refs[7]
    for source, target in zip(ins, state):
        target[...] = source[...]
    copy_all([two, three], joined)
    here = place[0]
    absorb_all(targets_of(here)[1:], last_segments(here)[:3], lambda i: q_peer, joined, state)
    state = [x.at[0] for x in state]
    lane = lax.broadcasted_iota(jnp.int32, (SPAN, HEAD_DIM), 1)
    for h in range(GROUP):
        rows = slice(h * SPAN, (h + 1) * SPAN)
        mass = jnp.sum(state[1][rows, :], axis=1, keepdims=True)
        safe = jnp.where(mass > 0.0, mass, 1.0)
        out[rows, :] = (state[2][rows, :] / safe).astype(BF)
        stats = jnp.zeros((SPAN, HEAD_DIM), F32)
        terms = three_terms(state[0][rows, :]) + three_terms(jnp.broadcast_to(mass, (SPAN, HEAD_DIM)))
        for i, term in enumerate(terms):
            stats = jnp.where(lane == i, term.astype(F32), stats)
        stats = stats.T
        both = jnp.concatenate([stats[:8, :HEAD_DIM], stats[:8, HEAD_DIM:]], axis=0)
        out[ROWS + 16 * h:ROWS + 16 * (h + 1), :] = both.astype(BF)


def own_kernel(place, q_own, two, three, near, before, *refs):
    ins, outs, joined = refs[:3], refs[3:6], refs[6]
    for source, target in zip(ins, outs):
        target[...] = source[0:1]
    copy_all([two, three, near], joined)
    here = place[0]
    absorb_all(targets_of(here)[:1], last_segments(here), lambda i: q_own, joined, outs)


def merge(top, total, summed, part, out):
    for h in range(GROUP):
        rows = slice(h * SPAN, (h + 1) * SPAN)
        both = part[ROWS + 16 * h:ROWS + 16 * (h + 1), :].astype(F32)
        stats = jnp.concatenate([both[:8, :], both[8:, :]], axis=1)
        stats = jnp.concatenate([stats, jnp.zeros((HEAD_DIM - 8, SPAN), F32)], axis=0).T
        other_top = stats[:, 0:1] + stats[:, 1:2] + stats[:, 2:3]
        other_mass = stats[:, 3:4] + stats[:, 4:5] + stats[:, 5:6]
        own_top = top[rows, :][:, 0:1]
        own_mass = jnp.sum(total[rows, :], axis=1, keepdims=True)
        peak = jnp.maximum(own_top, other_top)
        own_scale = jnp.exp2((own_top - peak) * SCALE)
        other_scale = jnp.exp2((other_top - peak) * SCALE) * other_mass
        norm = 1.0 / (own_mass * own_scale + other_scale)
        value = summed[rows, :] * (own_scale * norm) + part[rows, :].astype(F32) * (other_scale * norm)
        out[:, h * HEAD_DIM:(h + 1) * HEAD_DIM] = value.astype(BF)


def merge_kernel(top, total, summed, part, out, attended):
    merge(top.at[0], total.at[0], summed.at[0], part, attended)
    for t in range(TP):
        out[t] = attended[...]


def project_kernel(attended, weight, out):
    rows = jnp.concatenate([attended[t] for t in range(TP)], axis=1)
    total = jnp.dot(rows, weight[...].reshape(rows.shape[1], out.shape[1]), preferred_element_type=F32)
    out[...] = total.astype(BF)


def call(kernel, outs, operands, flops, scratch=(), smem_first=True):
    specs = [VMEM] * len(operands)
    if smem_first:
        specs[0] = SMEM
    nbytes = sum(int(np.prod(x.shape)) * x.dtype.itemsize for x in list(operands) + list(outs))
    result = pl.pallas_call(
        kernel,
        out_shape=tuple(outs),
        in_specs=specs,
        out_specs=tuple([VMEM] * len(outs)),
        scratch_shapes=list(scratch),
        compiler_params=pltpu.CompilerParams(vmem_limit_bytes=18 * 1024 * 1024),
        cost_estimate=pl.CostEstimate(flops=flops, bytes_accessed=nbytes, transcendentals=0),
    )(*operands)
    return result


def shape(dims, dtype):
    return jax.ShapeDtypeStruct(dims, dtype)


def z_route(core0, core1):
    route = []
    for z in range(N_Z):
        for r in range(4):
            d = core1 if r % 2 else core0
            route.append((z * 4 + r, ((z + d) % N_Z) * 4 + r))
    return route


SWAP_CORE = [(i, i ^ 1) for i in range(CTX)]
SWAP_HI = [(i, i ^ 2) for i in range(CTX)]
FAR_GROUPS = [
    [a * 16 + r for a in (range(N_ZH) if r % 2 == 0 else reversed(range(N_ZH)))] for r in range(16)
]


def local(queries, keys, values, out_weight):
    own_table, succ_table, inter_table = (jnp.asarray(t) for t in rope_tables())
    place = lax.axis_index("ctx").astype(jnp.int32).reshape(1)

    kv, q_own, q_intra, blocks = prepare(queries, keys, values, own_table, succ_table, inter_table, out_weight)
    q_peer = lax.ppermute(q_own, "ctx", SWAP_HI)
    far = lax.all_gather(kv, "ctx", axis=0, tiled=True, axis_index_groups=FAR_GROUPS)
    far, q_peer, blocks = lax.optimization_barrier((far, q_peer, blocks))
    weight = lax.all_to_all(blocks, "tp", 0, 0)
    near = [
        lax.ppermute(far, "ctx", z_route(1, 1)),
        lax.ppermute(far, "ctx", z_route(-1, -1)),
        lax.ppermute(far, "ctx", z_route(2, -2)),
    ]
    far_other = lax.ppermute(far, "ctx", SWAP_CORE)
    far_other, *near[:2] = lax.optimization_barrier((far_other, *near[:2]))

    state_shapes = [shape((1, ROWS, HEAD_DIM), F32)] * 3
    both_shapes = [shape((2, ROWS, HEAD_DIM), F32)] * 3
    token = shape((8, HEAD_DIM), F32)
    tile = 4 * ROWS * SPAN * HEAD_DIM
    size = far.shape[0]
    q_scratch = pltpu.VMEM((2, 2, ROWS, HEAD_DIM), BF)

    *state, done = call(
        first_kernel, both_shapes + [token], [place, q_own, q_peer, q_intra, kv, far, far_other], 17 * tile,
        scratch=[q_scratch, pltpu.VMEM((2 * size, HEAD_DIM), BF)],
    )
    *state, done, joined = call(
        near_kernel, both_shapes + [token, shape((2 * size, HEAD_DIM), BF)],
        [place, q_own, q_peer, done] + near[:2] + state, 16 * tile, scratch=[q_scratch],
    )
    two = lax.ppermute(joined, "ctx", SWAP_CORE)
    third, done = lax.optimization_barrier((near[2], done))
    three = lax.ppermute(third, "ctx", SWAP_CORE)
    peers = call(near_peer_kernel, state_shapes, [place, q_peer, third] + state, 4 * tile)
    (part,) = call(
        peer_kernel, [shape((PART_ROWS, HEAD_DIM), BF)], [place, q_peer, two, three] + list(peers), 12 * tile,
        scratch=[pltpu.VMEM((1, ROWS, HEAD_DIM), F32)] * 3 + [pltpu.VMEM((3 * size, HEAD_DIM), BF)],
    )
    part_here = lax.ppermute(part, "ctx", SWAP_HI)
    own = call(
        own_kernel, state_shapes, [place, q_own, two, three, third, done] + state, 16 * tile,
        scratch=[pltpu.VMEM((4 * size, HEAD_DIM), BF)],
    )
    (attended,) = call(
        merge_kernel, [shape((TP, SPAN, GROUP * HEAD_DIM), BF)], list(own) + [part_here], 10 ** 6, smem_first=False,
        scratch=[pltpu.VMEM((SPAN, GROUP * HEAD_DIM), BF)],
    )
    attended, weight = lax.optimization_barrier((attended, weight))
    attended = lax.all_to_all(attended, "tp", 0, 0)
    depth, width = weight.shape[1:]
    (out,) = call(
        project_kernel, [shape((SPAN, width), BF)], [attended, weight], 2 * SPAN * depth * TP * width, smem_first=False
    )
    return out


def solution(mesh):
    placed = (P("ctx", "tp"), P("ctx", "tp"), P("ctx", "tp"), P("tp", None))
    return jax.shard_map(
        local, mesh=mesh, in_specs=placed, out_specs=P("ctx", "tp"), check_vma=False
    )
```

```python
import functools

import jax
import jax.numpy as jnp
import numpy as np
from jax import lax
from jax.experimental import pallas as pl
from jax.experimental.pallas import tpu as pltpu
from jax.sharding import PartitionSpec as P

HEAD_DIM = 128
SPAN = 256
WINDOW = 128
INTER_POS = 511
GROUP = 3
ROWS = GROUP * SPAN
ROPE_BASE = 10000000.0
FLOOR = -1e30
SCALE = float(np.log2(np.e) / np.sqrt(HEAD_DIM))
BF = jnp.bfloat16
F32 = jnp.float32
VMEM = pl.BlockSpec(memory_space=pltpu.VMEM)
SMEM = pl.BlockSpec(memory_space=pltpu.SMEM)
PART_ROWS = ROWS + 16 * GROUP

N_Z, N_ZH, N_ZL = 16, 4, 4
STEPS = (-1, 1, 2)
CTX = 64
TP = 8


def rope_tables():
    half = HEAD_DIM // 2
    freq = np.float32(ROPE_BASE) ** (-(np.arange(half, dtype=np.float32) * np.float32(2.0)) / np.float32(HEAD_DIM))
    freq = freq.astype(np.float32)

    def table(positions):
        angles = (positions.astype(np.float32)[:, None] * freq[None, :]).astype(np.float32)
        return np.concatenate([np.cos(angles), np.sin(angles)], axis=1).astype(np.float32)

    offset = np.arange(SPAN)
    succ = np.where(offset < WINDOW, SPAN + offset, INTER_POS)
    inter = np.full((8,), INTER_POS)
    return table(offset), table(succ), table(inter)


def full_tables(table):
    lane = lax.broadcasted_iota(jnp.int32, table.shape, 1)
    turned = pltpu.roll(table, HEAD_DIM // 2, 1)
    first = lane < HEAD_DIM // 2
    return jnp.where(first, table, turned), jnp.where(first, -turned, table)


def rotated(x, tables):
    return x * tables[0] + pltpu.roll(x, HEAD_DIM // 2, 1) * tables[1]


def prepare_kernel(queries, keys, values, own, succ, inter, weight, kv, q_pair, q_intra, blocks, sems):
    width = blocks.shape[2]
    copies = [
        pltpu.make_async_copy(weight.at[:, t * width:(t + 1) * width], blocks.at[t], sems.at[t]) for t in range(TP)
    ]
    for copy in copies:
        copy.start()
    own_tables = full_tables(own[...])
    kv[:SPAN, :] = rotated(keys[...].astype(F32), own_tables).astype(BF)
    kv[SPAN:, :] = values[...]
    succ_tables = full_tables(succ[...])
    inter_tables = [jnp.broadcast_to(t[0:1, :], (SPAN, HEAD_DIM)) for t in full_tables(inter[...])]
    for h in range(GROUP):
        x = queries[:, h * HEAD_DIM:(h + 1) * HEAD_DIM].astype(F32)
        rows = slice(h * SPAN, (h + 1) * SPAN)
        q_pair[0, rows, :] = rotated(x, inter_tables).astype(BF)
        q_pair[1, rows, :] = rotated(x, succ_tables).astype(BF)
        q_intra[rows, :] = rotated(x, own_tables).astype(BF)
    for copy in copies:
        copy.wait()


def prepare(*operands):
    def whole(x):
        return pl.BlockSpec(x.shape, lambda i: (0,) * len(x.shape))

    depth, width = operands[-1].shape[0], operands[-1].shape[1] // TP
    outs = (
        shape((2 * SPAN, HEAD_DIM), BF), shape((2, ROWS, HEAD_DIM), BF), shape((ROWS, HEAD_DIM), BF),
        shape((TP, depth, width), BF),
    )
    return pl.pallas_call(
        prepare_kernel,
        grid=(1,),
        out_shape=outs,
        in_specs=[whole(x) for x in operands[:-1]] + [pl.BlockSpec(memory_space=pl.ANY)],
        out_specs=tuple(whole(x) for x in outs),
        scratch_shapes=[pltpu.SemaphoreType.DMA((TP,))],
        compiler_params=pltpu.CompilerParams(vmem_limit_bytes=60 * 1024 * 1024),
        cost_estimate=pl.CostEstimate(flops=10 ** 6, bytes_accessed=2 ** 23, transcendentals=0),
    )(*operands)


def scores(q, k):
    return lax.dot_general(q, k, (((1,), (1,)), ((), ())), preferred_element_type=F32)


def absorb(state, q, k, v, mask=None):
    top, total, summed = state
    lanes = k.shape[0] // HEAD_DIM
    s = scores(q[...], k)
    if mask is not None:
        s = jnp.where(mask, s, FLOOR)
    peak = s[:, :HEAD_DIM]
    for i in range(1, lanes):
        peak = jnp.maximum(peak, s[:, i * HEAD_DIM:(i + 1) * HEAD_DIM])
    old = top[...]
    new = jnp.maximum(old, jnp.max(peak, axis=1, keepdims=True))
    base = new * SCALE
    fade = jnp.exp2(old * SCALE - base)
    parts = []
    mass = total[...] * fade
    for i in range(lanes):
        w = jnp.exp2(s[:, i * HEAD_DIM:(i + 1) * HEAD_DIM] * SCALE - base)
        if mask is not None:
            w = jnp.where(mask[:, i * HEAD_DIM:(i + 1) * HEAD_DIM], w, 0.0)
        mass = mass + w
        parts.append(w.astype(BF))
    w = jnp.concatenate(parts, axis=1)
    top[...] = new
    total[...] = mass
    summed[...] = summed[...] * fade + jnp.dot(w, v, preferred_element_type=F32)


def absorb_buffer(state, span, q_ref, buf, row, first, step):
    low = jnp.minimum(first, first + 3 * step)
    count = jnp.clip((span - 2 - low + 64) // 16 - 3, 0, 4)
    start = jnp.where(step > 0, 0, 4 - count)

    def block(j):
        return pl.multiple_of(row + j * (2 * SPAN), 2 * SPAN)

    for size in (4, 3):
        @pl.when(count == size)
        def _(size=size):
            k = jnp.concatenate([buf[pl.ds(block(start + j), SPAN), :] for j in range(size)], axis=0)
            v = jnp.concatenate(
                [buf[pl.ds(pl.multiple_of(block(start + j) + SPAN, SPAN), SPAN), :] for j in range(size)], axis=0)
            absorb(state, q_ref.at[0], k, v)

    def one(j, carry):
        distance = span - (first + step * j)

        @pl.when(jnp.logical_or(distance == 1, jnp.logical_and(distance >= 2, count < 3)))
        def _():
            kind = jnp.where(distance == 1, 1, 0)
            k = buf[pl.ds(block(j), SPAN), :]
            v = buf[pl.ds(pl.multiple_of(block(j) + SPAN, SPAN), SPAN), :]
            absorb(state, q_ref.at[kind], k, v)

        return carry

    lax.fori_loop(0, N_ZH, one, 0)


def spans_of(place, step, other):
    core = lax.rem(place, 2)
    which = 1 - core if other else core
    residue = lax.rem(place // 4 + step + N_Z, N_ZL)
    first = residue * 4 + lax.rem(place // 2, 2) * 2 + which
    return first + jnp.where(which == 1, 48, 0), jnp.where(which == 1, -16, 16)


def targets_of(place):
    return place, place + 2 - 4 * lax.rem(place // 2, 2)


def pick(values, i):
    result = values[-1]
    for j in range(len(values) - 2, -1, -1):
        result = jnp.where(i == j, values[j], result)
    return result


def absorb_all(targets, segments, q_of, buf, states):
    size = N_ZH * 2 * SPAN
    count = len(segments)

    def one(i, carry):
        target, segment = i // count, lax.rem(i, count)
        absorb_buffer(
            [x.at[target] for x in states], pick(targets, target), q_of(target), buf, segment * size,
            pick([first for first, _ in segments], segment), pick([step for _, step in segments], segment),
        )
        return carry

    lax.fori_loop(0, len(targets) * count, one, 0)


def copy_all(sources, target):
    at = 0
    for source in sources:
        target[at:at + source.shape[0]] = source[...]
        at += source.shape[0]


def first_kernel(place, q_own, q_peer, q_intra, kv, far, top, total, summed, done, q_all):
    done[...] = jnp.zeros(done.shape, F32)
    states = (top, total, summed)
    top[...] = jnp.full(top.shape, FLOOR, F32)
    total[...] = jnp.zeros(total.shape, F32)
    summed[...] = jnp.zeros(summed.shape, F32)
    q_all[0] = q_own[...]
    q_all[1] = q_peer[...]
    row = lax.broadcasted_iota(jnp.int32, (ROWS, SPAN), 0) % SPAN
    column = lax.broadcasted_iota(jnp.int32, (ROWS, SPAN), 1)
    absorb([x.at[0] for x in states], q_intra, kv[:SPAN, :], kv[SPAN:, :], mask=row >= column)
    here = place[0]
    absorb_all(targets_of(here), [spans_of(here, 0, False)], lambda i: q_all.at[i], far, states)


def near_kernel(place, q_own, q_peer, before, low, high, far_other, *refs):
    ins, states, (done, joined, q_all, buffers) = refs[:3], refs[3:6], refs[6:]
    done[...] = before[...]
    for source, target in zip(ins, states):
        target[...] = source[...]
    q_all[0] = q_own[...]
    q_all[1] = q_peer[...]
    copy_all([low, high], joined)
    copy_all([low, high, far_other], buffers)
    here = place[0]
    segments = [spans_of(here, step, False) for step in STEPS[:2]] + [spans_of(here, 0, True)]
    absorb_all(targets_of(here), segments, lambda i: q_all.at[i], buffers, states)


def near_peer_kernel(place, q_peer, near, *refs):
    ins, states = refs[:3], refs[3:6]
    for source, target in zip(ins, states):
        target[...] = source[1:2]
    here = place[0]
    absorb_all(targets_of(here)[1:], [spans_of(here, STEPS[2], False)], lambda i: q_peer, near, states)


def three_terms(x):
    hi = x.astype(BF)
    rest = x - hi.astype(F32)
    mid = rest.astype(BF)
    low = (rest - mid.astype(F32)).astype(BF)
    return hi, mid, low


def last_segments(place):
    return [spans_of(place, step, True) for step in STEPS] + [spans_of(place, STEPS[2], False)]


def peer_kernel(place, q_peer, two, three, *refs):
    ins, out, state, joined = refs[:3], refs[3], refs[4:7], refs[7]
    for source, target in zip(ins, state):
        target[...] = source[...]
    copy_all([two, three], joined)
    here = place[0]
    absorb_all(targets_of(here)[1:], last_segments(here)[:3], lambda i: q_peer, joined, state)
    state = [x.at[0] for x in state]
    lane = lax.broadcasted_iota(jnp.int32, (SPAN, HEAD_DIM), 1)
    for h in range(GROUP):
        rows = slice(h * SPAN, (h + 1) * SPAN)
        mass = jnp.sum(state[1][rows, :], axis=1, keepdims=True)
        safe = jnp.where(mass > 0.0, mass, 1.0)
        out[rows, :] = (state[2][rows, :] / safe).astype(BF)
        stats = jnp.zeros((SPAN, HEAD_DIM), F32)
        terms = three_terms(state[0][rows, :]) + three_terms(jnp.broadcast_to(mass, (SPAN, HEAD_DIM)))
        for i, term in enumerate(terms):
            stats = jnp.where(lane == i, term.astype(F32), stats)
        stats = stats.T
        both = jnp.concatenate([stats[:8, :HEAD_DIM], stats[:8, HEAD_DIM:]], axis=0)
        out[ROWS + 16 * h:ROWS + 16 * (h + 1), :] = both.astype(BF)


def own_kernel(place, q_own, two, three, near, before, *refs):
    ins, outs, joined = refs[:3], refs[3:6], refs[6]
    for source, target in zip(ins, outs):
        target[...] = source[0:1]
    copy_all([two, three, near], joined)
    here = place[0]
    absorb_all(targets_of(here)[:1], last_segments(here), lambda i: q_own, joined, outs)


def merge(top, total, summed, part, out):
    for h in range(GROUP):
        rows = slice(h * SPAN, (h + 1) * SPAN)
        both = part[ROWS + 16 * h:ROWS + 16 * (h + 1), :].astype(F32)
        stats = jnp.concatenate([both[:8, :], both[8:, :]], axis=1)
        stats = jnp.concatenate([stats, jnp.zeros((HEAD_DIM - 8, SPAN), F32)], axis=0).T
        other_top = stats[:, 0:1] + stats[:, 1:2] + stats[:, 2:3]
        other_mass = stats[:, 3:4] + stats[:, 4:5] + stats[:, 5:6]
        own_top = top[rows, :][:, 0:1]
        own_mass = jnp.sum(total[rows, :], axis=1, keepdims=True)
        peak = jnp.maximum(own_top, other_top)
        own_scale = jnp.exp2((own_top - peak) * SCALE)
        other_scale = jnp.exp2((other_top - peak) * SCALE) * other_mass
        norm = 1.0 / (own_mass * own_scale + other_scale)
        value = summed[rows, :] * (own_scale * norm) + part[rows, :].astype(F32) * (other_scale * norm)
        out[:, h * HEAD_DIM:(h + 1) * HEAD_DIM] = value.astype(BF)


def merge_kernel(top, total, summed, part, out, attended):
    merge(top.at[0], total.at[0], summed.at[0], part, attended)
    for t in range(TP):
        out[t] = attended[...]


def project_kernel(attended, weight, out):
    rows = jnp.concatenate([attended[t] for t in range(TP)], axis=1)
    total = jnp.dot(rows, weight[...].reshape(rows.shape[1], out.shape[1]), preferred_element_type=F32)
    out[...] = total.astype(BF)


def call(kernel, outs, operands, flops, scratch=(), smem_first=True):
    specs = [VMEM] * len(operands)
    if smem_first:
        specs[0] = SMEM
    nbytes = sum(int(np.prod(x.shape)) * x.dtype.itemsize for x in list(operands) + list(outs))
    result = pl.pallas_call(
        kernel,
        out_shape=tuple(outs),
        in_specs=specs,
        out_specs=tuple([VMEM] * len(outs)),
        scratch_shapes=list(scratch),
        compiler_params=pltpu.CompilerParams(vmem_limit_bytes=18 * 1024 * 1024),
        cost_estimate=pl.CostEstimate(flops=flops, bytes_accessed=nbytes, transcendentals=0),
    )(*operands)
    return result


def shape(dims, dtype):
    return jax.ShapeDtypeStruct(dims, dtype)


def z_route(core0, core1):
    route = []
    for z in range(N_Z):
        for r in range(4):
            d = core1 if r % 2 else core0
            route.append((z * 4 + r, ((z + d) % N_Z) * 4 + r))
    return route


SWAP_CORE = [(i, i ^ 1) for i in range(CTX)]
SWAP_HI = [(i, i ^ 2) for i in range(CTX)]
FAR_GROUPS = [
    [a * 16 + r for a in (range(N_ZH) if r % 2 == 0 else reversed(range(N_ZH)))] for r in range(16)
]


def local(queries, keys, values, out_weight):
    own_table, succ_table, inter_table = (jnp.asarray(t) for t in rope_tables())
    place = lax.axis_index("ctx").astype(jnp.int32).reshape(1)

    kv, q_own, q_intra, blocks = prepare(queries, keys, values, own_table, succ_table, inter_table, out_weight)
    q_peer = lax.ppermute(q_own, "ctx", SWAP_HI)
    far = lax.all_gather(kv, "ctx", axis=0, tiled=True, axis_index_groups=FAR_GROUPS)
    far, q_peer, blocks = lax.optimization_barrier((far, q_peer, blocks))
    weight = lax.all_to_all(blocks, "tp", 0, 0)
    near = [
        lax.ppermute(far, "ctx", z_route(1, 1)),
        lax.ppermute(far, "ctx", z_route(-1, -1)),
        lax.ppermute(far, "ctx", z_route(2, -2)),
    ]
    far_other = lax.ppermute(far, "ctx", SWAP_CORE)

    kv, *near[:2] = lax.optimization_barrier((kv, *near[:2]))

    state_shapes = [shape((1, ROWS, HEAD_DIM), F32)] * 3
    both_shapes = [shape((2, ROWS, HEAD_DIM), F32)] * 3
    token = shape((8, HEAD_DIM), F32)
    tile = 4 * ROWS * SPAN * HEAD_DIM
    size = far.shape[0]
    q_scratch = pltpu.VMEM((2, 2, ROWS, HEAD_DIM), BF)

    *state, done = call(
        first_kernel, both_shapes + [token], [place, q_own, q_peer, q_intra, kv, far], 9 * tile, scratch=[q_scratch])
    far_other, done = lax.optimization_barrier((far_other, done))
    *state, done, joined = call(
        near_kernel, both_shapes + [token, shape((2 * size, HEAD_DIM), BF)],
        [place, q_own, q_peer, done] + near[:2] + [far_other] + state, 24 * tile,
        scratch=[q_scratch, pltpu.VMEM((3 * size, HEAD_DIM), BF)],
    )
    two = lax.ppermute(joined, "ctx", SWAP_CORE)
    third, done = lax.optimization_barrier((near[2], done))
    three = lax.ppermute(third, "ctx", SWAP_CORE)
    peers = call(near_peer_kernel, state_shapes, [place, q_peer, third] + state, 4 * tile)
    (part,) = call(
        peer_kernel, [shape((PART_ROWS, HEAD_DIM), BF)], [place, q_peer, two, three] + list(peers), 12 * tile,
        scratch=[pltpu.VMEM((1, ROWS, HEAD_DIM), F32)] * 3 + [pltpu.VMEM((3 * size, HEAD_DIM), BF)],
    )
    part_here = lax.ppermute(part, "ctx", SWAP_HI)
    own = call(
        own_kernel, state_shapes, [place, q_own, two, three, third, done] + state, 16 * tile,
        scratch=[pltpu.VMEM((4 * size, HEAD_DIM), BF)],
    )
    (attended,) = call(
        merge_kernel, [shape((TP, SPAN, GROUP * HEAD_DIM), BF)], list(own) + [part_here], 10 ** 6, smem_first=False,
        scratch=[pltpu.VMEM((SPAN, GROUP * HEAD_DIM), BF)],
    )
    attended, weight = lax.optimization_barrier((attended, weight))
    attended = lax.all_to_all(attended, "tp", 0, 0)
    depth, width = weight.shape[1:]
    (out,) = call(
        project_kernel, [shape((SPAN, width), BF)], [attended, weight], 2 * SPAN * depth * TP * width, smem_first=False
    )
    return out


def solution(mesh):
    placed = (P("ctx", "tp"), P("ctx", "tp"), P("ctx", "tp"), P("tp", None))
    return jax.shard_map(
        local, mesh=mesh, in_specs=placed, out_specs=P("ctx", "tp"), check_vma=False
    )
```
